32 devices in a mesh: groups: 2 (over x), vocab: 16 (over z, y, core).
Axes of the slice: x: 2, y: 2, z: 4, core: 2. Of those that a mesh axis runs over, the one named last changes fastest.
Arguments:
- hidden: bfloat16 [8192, 3584], P(('groups', 'vocab')), parts along dimension 0, may hold values from -6 to 6
- head_weight: bfloat16 [76032, 3584], P('vocab'), may hold values from -0.29882812 to 0.29882812
- term_grad: float32 [32, 76032], P('groups', 'vocab'), parts along dimension 0, may hold values from -24 to 24
- winner: int32 [32, 76032], P('groups', 'vocab'), parts along dimension 0, may hold values from 0 to 63
- route: int32 [2048, 2], P(('groups', 'vocab')), parts along dimension 0, may hold values from 0 to 15, all different within a row; in each aligned block of 64 rows (0 to 63, 64 to 127, ...) at most 16 rows name the same one
Outputs:
- weight_grad: bfloat16 [152064, 3584], P(('groups', 'vocab')), parts along dimension 0
- hidden_grad: bfloat16 [8192, 3584], P(('groups', 'vocab')), parts along dimension 0
The draws below stay inside these ranges and needn't reach their ends.
There are 2 independent parts, one for each index of `groups`. The reference program is written for one: setup_inputs(seed, part) draws one part's arguments, and reference() takes and returns one part's arrays. A program takes and returns all parts, laid end to end along the dimension named above; an argument that names none is the same for every part. Nothing has to cross between parts.
Inputs may be any that keep to these rules, and one draw needn't show every extreme that they name: `winner`: A code is a slot c of the document's blocks listed for the entry's tile times 4 plus a position in that block; codes whose slot is not filled name no token. `route`: each block names 2 different tiles; among the blocks of one document at most 16 name the same tile, and in every draw some tile is named by exactly 16 blocks of some document.
All inputs are finite; a program needn't handle non-finite values.
Results may differ from the reference program's by a relative error of at most 0.0059.
Values may be sent and summed in bfloat16 or wider, within the bound.
A program may use at most 256 MiB of HBM per device.

```python
import math
import jax
import jax.numpy as jnp
import numpy as np
from jax import lax

D = 3584
V = 76032
BLOCK = 4
TOP = 2
DOCS = 16
TOKENS = 4096
NB_DOC = 64
NBLK = 1024
VT = 4752
CAP = 16
N_VOCAB = 16


def plant(entries, own_key, smallest, top_value):
    extent = entries.shape
    spot = [jax.random.randint(jax.random.fold_in(own_key, axis), (), 0, extent[axis]) for axis in range(len(extent))]
    entries = entries.at[tuple(spot)].set(smallest)
    longest = extent.index(max(extent))
    spot[longest] = (spot[longest] + 1) % extent[longest]
    return entries.at[tuple(spot)].set(top_value)


def shard_levels(rng, dims, pieces, low, high):
    factor_of, own = 1.0, jax.random.fold_in(rng, 6)
    for dim, parts in pieces:
        draws = jnp.exp(jax.random.uniform(jax.random.fold_in(own, dim), (parts,), jnp.float32, low / len(pieces), high / len(pieces)))
        factor_of = factor_of * jnp.repeat(draws, dims[dim] // parts).reshape([-1 if axis == dim else 1 for axis in range(len(dims))])
    return factor_of


def shared_out(rng, own, number, rows, number_of, top, most, lean):
    order = jax.random.permutation(rng, number_of)
    heavy_load, common = shares(number_of, rows * top, most, lean, True), shares(number_of, rows * top, most, lean, False)
    places = jnp.arange(number_of)

    def named(sizes, offset_by):
        used = int((sizes > 0).sum())
        fixed = max(1, used // 4)
        passed = fixed + (places - fixed + offset_by * (used - fixed)) % max(1, number_of - fixed)
        return jnp.zeros((number_of,), jnp.int32).at[order[jnp.where(places < fixed, places, passed)]].set(jnp.asarray(sizes, jnp.int32))

    sizes = jnp.where(number % 4 == 0, named(heavy_load, number // 4), named(common, number - number // 4 - 1))
    mixed = jax.random.permutation(jax.random.fold_in(own, 3), number_of)
    giver, sink = mixed[0:number_of // 2 * 2:2], mixed[1:number_of // 2 * 2:2]
    slack = jnp.minimum(sizes[giver] - 1, most - sizes[sink]) // 2
    slack = jnp.where((giver == order[0]) | (sink == order[0]) | (sizes[sink] == 0), 0, jnp.maximum(slack, 0))
    passed = jax.random.randint(jax.random.fold_in(own, 4), (number_of // 2,), 0, 1 << 20) % (slack + 1)
    sizes = sizes.at[giver].add(-passed).at[sink].add(passed)
    labels = jnp.searchsorted(jnp.cumsum(sizes), jnp.arange(rows * top), side="right").astype(jnp.int32)
    grid = labels.reshape(top, rows).T
    grid = grid[jax.random.permutation(jax.random.fold_in(own, 1), rows)]
    offset_by = jax.random.randint(jax.random.fold_in(own, 2), (rows, 1), 0, top)
    return jnp.take_along_axis(grid, (jnp.arange(top)[None, :] + offset_by) % top, axis=1)


def shares(count, total, bound, skew, full):
    portions = [(1 << 20) // math.isqrt(grade ** skew) + 1 for grade in range(1, count + 1)]
    largest = bound if full else min(bound, max(-(-total // count), total * portions[0] // sum(portions)))
    least = 1 if total - largest >= count - 1 else 0
    counts, rest = [largest] + [least] * (count - 1), total - largest - least * (count - 1)
    while rest > 0:
        free = [i for i in range(1, count) if counts[i] < largest] or [i for i in range(1, count) if counts[i] < bound]
        mass, left = sum([portions[i] for i in free]), rest
        for i in free:
            more = min(bound - counts[i], max(1, left * portions[i] // mass), rest)
            counts[i] = counts[i] + more
            rest = rest - more
    return np.array(counts)


def normal_values(rng, extent, spread, most, split=(), held_as=jnp.bfloat16):
    entries = jax.random.normal(rng, extent, jnp.float32) * spread
    if len(split) > 0:
        entries = shard_levels(rng, extent, split, -0.22, 0.18) * entries
    return jnp.clip(entries, min=-most, max=most).astype(held_as)


def setup_inputs(seed: int = 0, part: int = 0) -> dict:
    keys = jax.random.split(jax.random.key(seed), 6)
    own_keys = jax.random.split(jax.random.fold_in(keys[5], part), 6)
    hidden = normal_values(own_keys[0], (TOKENS, D), 1.0, 6.0, ((0, 16),))
    head_weight = normal_values(keys[1], (V, D), 0.05, 0.29882812, ((0, 16),))
    term_grad = normal_values(own_keys[2], (DOCS, V), 4.0, 24.0, ((1, 16),), jnp.float32)
    winner = plant(jax.random.randint(own_keys[3], (DOCS, V), 0, CAP * BLOCK), jax.random.fold_in(own_keys[3], 1), 0, (CAP * BLOCK) - 1).astype(jnp.int32)
    route_keys = jax.random.split(jax.random.fold_in(own_keys[4], 1), NBLK // NB_DOC)
    route_turns = jax.random.permutation(jax.random.fold_in(own_keys[4], 3), NBLK // NB_DOC)
    route = jax.vmap(lambda own, number: shared_out(jax.random.fold_in(own_keys[4], 2), own, number, NB_DOC, N_VOCAB, TOP, CAP, 2))(route_keys, route_turns).reshape((NBLK, TOP))
    return dict(hidden=hidden, head_weight=head_weight, term_grad=term_grad, winner=winner, route=route)


def saturation_slope(logits):
    return jax.nn.sigmoid(logits) / (1.0 + jax.nn.softplus(logits))


def reference(hidden, head_weight, term_grad, winner, route):
    token_blocks = hidden.reshape(DOCS, NB_DOC, BLOCK * D)
    doc_routes = route.reshape(DOCS, NB_DOC, TOP)
    slot_codes = jnp.arange(CAP * BLOCK, dtype=jnp.int32)
    slot_ids = jnp.arange(CAP, dtype=jnp.int32)
    positions = jnp.arange(NB_DOC, dtype=jnp.int32)

    def take_rows(block_rows, source):
        return jnp.take(block_rows, source, axis=0)

    def one_tile(running, tile_index):
        listed = jnp.any(doc_routes == tile_index, axis=2).astype(jnp.int32)
        ranking = jnp.cumsum(listed, axis=1) - 1
        picked = (listed[:, :, None] == 1) & (ranking[:, :, None] == slot_ids[None, None, :])
        source = jnp.sum(jnp.where(picked, positions[None, :, None], 0), axis=1).astype(jnp.int32)
        filled = jnp.any(picked, axis=1)
        gathered = jax.vmap(take_rows)(token_blocks, source)
        gathered = jnp.where(filled[:, :, None], gathered, jnp.zeros((), hidden.dtype))
        picked_rows = gathered.reshape(DOCS * CAP * BLOCK, D)
        start = (tile_index * VT).astype(jnp.int32)
        weight_tile = lax.dynamic_slice_in_dim(head_weight, start, VT, 0)
        grad_tile = lax.dynamic_slice_in_dim(term_grad, start, VT, 1)
        winner_tile = lax.dynamic_slice_in_dim(winner, start, VT, 1)
        logits = lax.dot_general(picked_rows, weight_tile, (((1,), (1,)), ((), ())), preferred_element_type=jnp.float32)
        logits = logits.reshape(DOCS, CAP * BLOCK, VT)
        live = (winner_tile[:, None, :] == slot_codes[None, :, None]) & jnp.repeat(filled, BLOCK, axis=1)[:, :, None]
        term_delta = jnp.where(live, grad_tile[:, None, :] * saturation_slope(logits), 0.0).astype(jnp.bfloat16)
        term_delta = term_delta.reshape(DOCS * CAP * BLOCK, VT)
        weight_part = lax.dot_general(term_delta, picked_rows, (((0,), (0,)), ((), ())), preferred_element_type=jnp.float32).astype(jnp.bfloat16)
        partial_value = jnp.dot(term_delta, weight_tile, preferred_element_type=jnp.float32).astype(jnp.bfloat16)
        partial_value = partial_value.reshape(DOCS, CAP, BLOCK * D)
        scattered = jnp.einsum("dnc,dcx->dnx", picked.astype(jnp.float32), partial_value.astype(jnp.float32))
        return running + scattered, weight_part

    running_zero = jnp.zeros((DOCS, NB_DOC, BLOCK * D), jnp.float32)
    total, weight_rows = lax.scan(one_tile, running_zero, jnp.arange(N_VOCAB, dtype=jnp.int32))
    weight_grad = weight_rows.reshape(V, D)
    hidden_grad = total.reshape(TOKENS, D).astype(jnp.bfloat16)
    return (weight_grad, hidden_grad)
```

```python
import functools

import jax
import jax.numpy as jnp
from jax import lax
from jax.experimental import pallas as pl
from jax.experimental.pallas import tpu as pltpu
from jax.sharding import PartitionSpec as P

BLOCK = 4
V_TILE = 512
OUT_CHUNKS = 2
BACK_CHUNKS = 2
PAIRED_MOST = 8
VMEM = 56 * 1024 * 1024


def saturation_slope(x):
    small = jnp.exp(-jnp.abs(x))
    softplus = jnp.maximum(x, 0.0) + jnp.log1p(small)
    sigmoid = jnp.where(x >= 0, 1.0, small) / (1.0 + small)
    return sigmoid / (1.0 + softplus)


def delta_kernel(docs, x_ref, w_ref, winner_ref, grad_ref, delta_ref):
    rows, width = delta_ref.shape
    logits = lax.dot_general(
        x_ref[...], w_ref[...], (((1,), (1,)), ((), ())), preferred_element_type=jnp.float32
    )
    logits = logits.reshape(docs, rows // docs, width)
    codes = lax.broadcasted_iota(jnp.int32, logits.shape, 1)
    chosen = winner_ref[...][:, None, :] == codes
    picked = jnp.sum(jnp.where(chosen, logits, 0.0), axis=1)
    delta = grad_ref[...] * saturation_slope(picked)
    spread = jnp.where(chosen, delta[:, None, :], 0.0)
    delta_ref[...] = spread.reshape(rows, width).astype(jnp.bfloat16)


def term_deltas(rows, weight, winner, grad):
    count, width = rows.shape
    vocab = weight.shape[0]
    docs = winner.shape[0]
    return pl.pallas_call(
        functools.partial(delta_kernel, docs),
        grid=(pl.cdiv(vocab, V_TILE),),
        in_specs=[
            pl.BlockSpec((count, width), lambda i: (0, 0)),
            pl.BlockSpec((V_TILE, width), lambda i: (i, 0)),
            pl.BlockSpec((docs, V_TILE), lambda i: (0, i)),
            pl.BlockSpec((docs, V_TILE), lambda i: (0, i)),
        ],
        out_specs=pl.BlockSpec((count, V_TILE), lambda i: (0, i)),
        out_shape=jax.ShapeDtypeStruct((count, vocab), jnp.bfloat16),
        compiler_params=pltpu.CompilerParams(vmem_limit_bytes=VMEM),
        cost_estimate=pl.CostEstimate(
            flops=2 * count * vocab * width,
            bytes_accessed=2 * vocab * width + 2 * count * (vocab + width),
            transcendentals=0,
        ),
        name="term_deltas",
    )(rows, weight, winner, grad)


def weight_kernel(da_ref, db_ref, xa_ref, xb_ref, out_ref):
    dims = (((0,), (0,)), ((), ()))
    total = lax.dot_general(da_ref[...], xa_ref[...], dims, preferred_element_type=jnp.float32)
    total += lax.dot_general(db_ref[...], xb_ref[...], dims, preferred_element_type=jnp.float32)
    out_ref[...] = total.astype(jnp.bfloat16)


def weight_grads(delta_a, delta_b, rows_a, rows_b):
    count, vocab = delta_a.shape
    width = rows_a.shape[1]
    whole = pl.BlockSpec((count, width), lambda i: (0, 0))
    part = pl.BlockSpec((count, V_TILE), lambda i: (0, i))
    return pl.pallas_call(
        weight_kernel,
        grid=(pl.cdiv(vocab, V_TILE),),
        in_specs=[part, part, whole, whole],
        out_specs=pl.BlockSpec((V_TILE, width), lambda i: (i, 0)),
        out_shape=jax.ShapeDtypeStruct((vocab, width), jnp.bfloat16),
        compiler_params=pltpu.CompilerParams(vmem_limit_bytes=VMEM),
        cost_estimate=pl.CostEstimate(
            flops=4 * count * vocab * width,
            bytes_accessed=2 * vocab * width + 4 * count * (vocab + width),
            transcendentals=0,
        ),
        name="weight_grads",
    )(delta_a, delta_b, rows_a, rows_b)


TILE = 256
RELAY_CHUNKS = 2
BACK_WIDTH = 512
MESH = pl.DeviceIdType.MESH


def fused_kernel(
    hidden, near_pick, far_pick, winner, grad, weight,
    weight_grad, hidden_grad,
    relay, near_out, far_out, rows, delta, w_tiles, w_columns, g_tiles, landing, back_out, back_in,
    relay_send, relay_recv, near_send, near_recv, far_send, far_recv,
    home_send, home_recv, part_send, part_recv, back_send, back_recv, tile_sem, column_sem, grad_sem,
):
    tokens, width = hidden.shape
    vocab = weight.shape[0]
    tiles, docs, _ = winner.shape
    near_docs = docs // 2
    count = near_out.shape[0]
    slot = count // near_docs
    peers = near_docs
    me = lax.axis_index("vocab")
    side = me // peers
    local = me % peers
    across = (me + peers) % (2 * peers)
    overlap = tiles * TILE - vocab

    def peer(k):
        flipped, scale = 0, 1
        while scale < peers:
            bit = local // scale % 2
            flipped = flipped + scale * ((1 - bit) if k & scale else bit)
            scale *= 2
        return side * peers + flipped

    def send(src, dst, send_sem, recv_sem, device):
        return pltpu.make_async_remote_copy(
            src_ref=src, dst_ref=dst, send_sem=send_sem, recv_sem=recv_sem,
            device_id={"vocab": device}, device_id_type=MESH,
        )

    def slots(k):
        return pl.ds(k * slot, slot)

    barrier = pltpu.get_barrier_semaphore()
    for k in range(1, peers):
        pl.semaphore_signal(barrier, inc=1, device_id={"vocab": peer(k)}, device_id_type=MESH)
    pl.semaphore_signal(barrier, inc=1, device_id={"vocab": across}, device_id_type=MESH)
    pl.semaphore_wait(barrier, peers)

    relay_width = width // RELAY_CHUNKS
    relays = []
    for c in range(RELAY_CHUNKS):
        part = pl.ds(c * relay_width, relay_width)
        relays.append(
            send(hidden.at[:, part], relay.at[:, part], relay_send.at[c], relay_recv.at[c], across)
        )
        relays[c].start()

    def tile_copy(i, place):
        start = pl.multiple_of(i * TILE - i // (tiles - 1) * overlap, 16)
        return pltpu.make_async_copy(
            weight.at[pl.ds(start, TILE), :], w_tiles.at[place], tile_sem.at[place]
        )

    def column_copies(j, place):
        columns = pl.ds(pl.multiple_of(j * TILE, TILE), TILE)
        full = (tiles - 1) * TILE
        return (
            pltpu.make_async_copy(
                weight.at[pl.ds(0, full), columns],
                w_columns.at[place, pl.ds(0, full), :],
                column_sem.at[place, 0],
            ),
            pltpu.make_async_copy(
                weight.at[pl.ds(vocab - TILE, TILE), columns],
                w_columns.at[place, pl.ds(full, TILE), :],
                column_sem.at[place, 1],
            ),
        )

    def start_columns(j, place):
        for copy in column_copies(j, place):
            copy.start()

    near_out[...] = jnp.dot(
        near_pick[...], hidden[...], preferred_element_type=jnp.float32
    ).astype(jnp.bfloat16)
    near_sends = []
    for k in range(1, peers):
        copy = send(
            near_out.at[slots(k), :], rows.at[slots(k), :], near_send.at[k], near_recv.at[k], peer(k)
        )
        copy.start()
        near_sends.append(copy)
    rows[pl.ds(0, slot), :] = near_out[pl.ds(0, slot), :]

    far_sends = []

    def pass_on(c):
        relays[c].wait_recv()
        part = pl.ds(c * relay_width, relay_width)
        far_out[:, part] = jnp.dot(
            far_pick[...], relay[:, part], preferred_element_type=jnp.float32
        ).astype(jnp.bfloat16)
        for k in range(1, peers):
            copy = send(
                far_out.at[slots(k), part],
                rows.at[pl.ds(count + k * slot, slot), part],
                far_send.at[c, k],
                far_recv.at[c, k],
                peer(k),
            )
            copy.start()
            far_sends.append(copy)
        rows[pl.ds(count, slot), part] = far_out[pl.ds(0, slot), part]

    def deltas(row, doc):
        tile_copy(0, 0).start()

        def body(i, carry):
            place = i % 2

            @pl.when(i + 1 < tiles)
            def _():
                tile_copy(i + 1, 1 - place).start()

            tile_copy(i, place).wait()
            logits = lax.dot_general(
                rows[pl.ds(row, count), :],
                w_tiles[place],
                (((1,), (1,)), ((), ())),
                preferred_element_type=jnp.float32,
            )
            logits = logits.reshape(near_docs, slot, TILE)
            codes = lax.broadcasted_iota(jnp.int32, logits.shape, 1)
            chosen = winner[i, pl.ds(doc, near_docs), :][:, None, :] == codes
            picked = jnp.sum(jnp.where(chosen, logits, 0.0), axis=1)
            term = grad[i, pl.ds(doc, near_docs), :] * saturation_slope(picked)
            spread = jnp.where(chosen, term[:, None, :], 0.0)
            delta[pl.ds(row, count), pl.ds(pl.multiple_of(i * TILE, TILE), TILE)] = spread.reshape(
                count, TILE
            ).astype(jnp.bfloat16)
            return carry

        lax.fori_loop(0, tiles, body, 0)

    columns = width // TILE

    def column_step(row, j, out, home):
        place = j % 2

        @pl.when(j + 1 < columns)
        def _():
            start_columns(j + 1, 1 - place)

        for copy in column_copies(j, place):
            copy.wait()
        value = jnp.dot(
            delta[pl.ds(row, count), :], w_columns[place], preferred_element_type=jnp.float32
        ).astype(jnp.bfloat16)
        where = pl.ds(pl.multiple_of(j * TILE, TILE), TILE)
        out[:, where] = value
        landing[home, pl.ds(0, slot), where] = value[:slot]

    pass_on(0)
    for copy in near_sends:
        copy.wait_recv()
    start_columns(0, 0)
    deltas(0, 0)
    for c in range(1, RELAY_CHUNKS):
        pass_on(c)
    for copy in near_sends:
        copy.wait_send()

    def near_column(j, carry):
        column_step(0, j, near_out, 0)
        return carry

    lax.fori_loop(0, columns, near_column, 0)
    start_columns(0, 0)
    for copy in far_sends:
        copy.wait_recv()
    homes = []
    for k in range(1, peers):
        copy = send(
            near_out.at[slots(k), :],
            landing.at[0, slots(k), :],
            home_send.at[k],
            home_recv.at[k],
            peer(k),
        )
        copy.start()
        homes.append(copy)
    deltas(count, near_docs)
    for copy in far_sends:
        copy.wait_send()
    per_chunk = BACK_WIDTH // TILE
    chunks = width // BACK_WIDTH

    def part_copy(c, k):
        part = pl.ds(pl.multiple_of(c * BACK_WIDTH, BACK_WIDTH), BACK_WIDTH)
        return send(
            far_out.at[slots(k), part],
            landing.at[1, slots(k), part],
            part_send.at[c, k],
            part_recv.at[c, k],
            peer(k),
        )

    def far_columns(c, carry):
        for t in range(per_chunk):
            column_step(count, c * per_chunk + t, far_out, 1)
        for k in range(1, peers):
            part_copy(c, k).start()
        return carry

    lax.fori_loop(0, chunks, far_columns, 0)

    def back_copy(c):
        part = pl.ds(pl.multiple_of(c * BACK_WIDTH, BACK_WIDTH), BACK_WIDTH)
        return send(
            back_out.at[:, part], back_in.at[:, part], back_send.at[c], back_recv.at[c], across
        )

    gather = (((0,), (0,)), ((), ()))

    def pass_back(c):
        for k in range(1, peers):
            part_copy(c, k).wait()
        part = pl.ds(pl.multiple_of(c * BACK_WIDTH, BACK_WIDTH), BACK_WIDTH)
        back_out[:, part] = lax.dot_general(
            far_pick[...], landing[1, :, part], gather, preferred_element_type=jnp.float32
        ).astype(jnp.bfloat16)
        back_copy(c).start()

    def grad_copy(i, place):
        start = pl.multiple_of(i * TILE, TILE)
        return pltpu.make_async_copy(
            g_tiles.at[place], weight_grad.at[pl.ds(start, TILE), :], grad_sem.at[place]
        )

    def grad_tile(i):
        return lax.dot_general(
            delta[:, pl.ds(pl.multiple_of(i * TILE, TILE), TILE)],
            rows[...],
            gather,
            preferred_element_type=jnp.float32,
        ).astype(jnp.bfloat16)

    def grad_body(i, carry):
        place = i % 2

        @pl.when(i >= 2)
        def _():
            grad_copy(i - 2, place).wait()

        g_tiles[place] = grad_tile(i)
        grad_copy(i, place).start()

        @pl.when((i % 2 == 1) & (i // 2 < chunks))
        def _():
            pass_back(i // 2)

        return carry

    lax.fori_loop(0, tiles - 1, grad_body, 0)
    last = tiles - 1
    grad_copy(last - 2, last % 2).wait()
    g_tiles[last % 2] = grad_tile(last)
    tail = pltpu.make_async_copy(
        g_tiles.at[last % 2, pl.ds(overlap, TILE - overlap), :],
        weight_grad.at[pl.ds(last * TILE, TILE - overlap), :],
        grad_sem.at[last % 2],
    )
    tail.start()
    for copy in homes:
        copy.wait()

    def finish(c, carry):
        back_copy(c).wait()
        part = pl.ds(pl.multiple_of(c * BACK_WIDTH, BACK_WIDTH), BACK_WIDTH)
        own = lax.dot_general(
            near_pick[...], landing[0, :, part], gather, preferred_element_type=jnp.float32
        )
        hidden_grad[:, part] = (own + back_in[:, part].astype(jnp.float32)).astype(jnp.bfloat16)
        return carry

    lax.fori_loop(0, chunks, finish, 0)
    for copy in relays:
        copy.wait_send()
    grad_copy(last - 1, (last - 1) % 2).wait()
    tail.wait()


def fused(hidden, near_pick, far_pick, winner, grad, weight):
    tokens, width = hidden.shape
    vocab = weight.shape[0]
    count = near_pick.shape[0]
    tiles, docs, _ = winner.shape
    peers = docs // 2
    chunks = width // BACK_WIDTH
    held = jnp.bfloat16
    dma = pltpu.SemaphoreType.DMA
    vmem = pl.BlockSpec(memory_space=pltpu.VMEM)
    hbm = pl.BlockSpec(memory_space=pl.ANY)
    return pl.pallas_call(
        fused_kernel,
        in_specs=[vmem] * 5 + [hbm],
        out_specs=[hbm, vmem],
        out_shape=[
            jax.ShapeDtypeStruct((vocab, width), held),
            jax.ShapeDtypeStruct((tokens, width), held),
        ],
        scratch_shapes=[
            pltpu.VMEM((tokens, width), held),
            pltpu.VMEM((count, width), held),
            pltpu.VMEM((count, width), held),
            pltpu.VMEM((2 * count, width), held),
            pltpu.VMEM((2 * count, tiles * TILE), held),
            pltpu.VMEM((2, TILE, width), held),
            pltpu.VMEM((2, tiles * TILE, TILE), held),
            pltpu.VMEM((2, TILE, width), held),
            pltpu.VMEM((2, count, width), held),
            pltpu.VMEM((tokens, width), held),
            pltpu.VMEM((tokens, width), held),
            dma((RELAY_CHUNKS,)), dma((RELAY_CHUNKS,)),
            dma((peers,)), dma((peers,)),
            dma((RELAY_CHUNKS, peers)), dma((RELAY_CHUNKS, peers)),
            dma((peers,)), dma((peers,)),
            dma((chunks, peers)), dma((chunks, peers)),
            dma((chunks,)), dma((chunks,)),
            dma((2,)), dma((2, 2)), dma((2,)),
        ],
        compiler_params=pltpu.CompilerParams(
            collective_id=0, has_side_effects=True, vmem_limit_bytes=62 * 1024 * 1024
        ),
        name="fused",
    )(hidden, near_pick, far_pick, winner, grad, weight)


def tiled(x, blank):
    vocab = x.shape[1]
    tiles = pl.cdiv(vocab, TILE)
    full = (tiles - 1) * TILE
    tail = x[:, vocab - TILE :]
    if blank:
        fresh = jnp.arange(TILE) >= tiles * TILE - vocab
        tail = jnp.where(fresh[None, :], tail, 0)
    whole = jnp.concatenate([x[:, :full], tail], axis=1)
    return whole.reshape(x.shape[0], tiles, TILE).swapaxes(0, 1)


def on_device(hidden, head_weight, term_grad, winner, route):
    n = lax.axis_size("vocab")
    half = n // 2
    me = lax.axis_index("vocab")
    tokens, width = hidden.shape
    block_count = route.shape[0]
    capacity = 2 * max(1, block_count * route.shape[1] // n)
    slot_rows = capacity * BLOCK
    base = me // half * half
    peers = jnp.arange(half, dtype=jnp.int32)
    paired = half <= PAIRED_MOST and half & (half - 1) == 0
    if paired:
        peers = peers ^ (me % half)
    near, far = base + peers, (half - base) + peers

    def cross(x):
        return lax.ppermute(x, "vocab", [(i, (i + half) % n) for i in range(n)])

    def exchange(pieces):
        if not paired:
            sides = [list(range(half)), list(range(half, n))]
            return list(lax.all_to_all(pieces, "vocab", 0, 0, axis_index_groups=sides, tiled=True))
        pieces = list(pieces)
        return [pieces[0]] + [
            lax.ppermute(pieces[k], "vocab", [(i, i ^ k) for i in range(n)])
            for k in range(1, half)
        ]

    def chooser(table):
        listed = jnp.any(table[:, :, None] == near[None, None, :], axis=1)
        ranking = jnp.cumsum(listed.astype(jnp.int32), axis=0) - 1
        slot = jnp.where(listed, ranking, -1)
        slots = jnp.arange(half * slot_rows, dtype=jnp.int32)
        place = jnp.arange(tokens, dtype=jnp.int32)
        wanted = jnp.repeat(jnp.repeat(slot.T, BLOCK, axis=1), slot_rows, axis=0)
        match = wanted == (slots % slot_rows // BLOCK)[:, None]
        match &= (slots % BLOCK)[:, None] == (place % BLOCK)[None, :]
        return match.astype(jnp.bfloat16)

    def select(pick, rows):
        chosen = jnp.dot(pick, rows, preferred_element_type=jnp.float32).astype(jnp.bfloat16)
        return chosen.reshape(half, slot_rows, rows.shape[1])

    def gather_back(pick, parts):
        return lax.dot_general(
            pick,
            jnp.concatenate(parts, axis=0),
            (((0,), (0,)), ((), ())),
            preferred_element_type=jnp.float32,
        )

    out_step = width // OUT_CHUNKS
    back_step = width // BACK_CHUNKS
    far_route = cross(route)
    near_pick, far_pick = chooser(route), chooser(far_route)
    if paired and slot_rows % 16 == 0:
        order = jnp.concatenate([near, far])
        return tuple(
            fused(
                hidden,
                near_pick,
                far_pick,
                tiled(winner[order], False),
                tiled(term_grad[order], True),
                head_weight,
            )
        )
    far_hidden = [cross(hidden[:, c * out_step : (c + 1) * out_step]) for c in range(OUT_CHUNKS)]
    near_rows = jnp.concatenate(exchange(select(near_pick, hidden)), axis=0)
    far_rows = [
        jnp.concatenate(exchange(select(far_pick, piece)), axis=0) for piece in far_hidden
    ]
    far_rows = jnp.concatenate(far_rows, axis=1)

    near_delta = term_deltas(near_rows, head_weight, winner[near], term_grad[near])
    far_delta = term_deltas(far_rows, head_weight, winner[far], term_grad[far])

    def parts(delta, c):
        value = jnp.dot(
            delta,
            head_weight[:, c * back_step : (c + 1) * back_step],
            preferred_element_type=jnp.float32,
        ).astype(jnp.bfloat16)
        return exchange(value.reshape(half, slot_rows, back_step))

    far_sum = [
        cross(gather_back(far_pick, parts(far_delta, c)).astype(jnp.bfloat16))
        for c in range(BACK_CHUNKS)
    ]
    near_sum = [gather_back(near_pick, parts(near_delta, c)) for c in range(BACK_CHUNKS)]
    hidden_grad = jnp.concatenate(
        [
            (a + b.astype(jnp.float32)).astype(jnp.bfloat16)
            for a, b in zip(near_sum, far_sum)
        ],
        axis=1,
    )
    weight_grad = weight_grads(near_delta, far_delta, near_rows, far_rows)
    return (weight_grad, hidden_grad)


def solution(mesh):
    placed = (
        P(("groups", "vocab"), None),
        P("vocab", None),
        P("groups", "vocab"),
        P("groups", "vocab"),
        P(("groups", "vocab"), None),
    )
    return jax.shard_map(
        on_device,
        mesh=mesh,
        in_specs=placed,
        out_specs=(P(("groups", "vocab"), None), P(("groups", "vocab"), None)),
        check_vma=False,
    )
```

```python
import functools

import jax
import jax.numpy as jnp
from jax import lax
from jax.experimental import pallas as pl
from jax.experimental.pallas import tpu as pltpu
from jax.sharding import PartitionSpec as P

BLOCK = 4
TOP = 2
V_TILE = 512
OUT_CHUNKS = 2
BACK_CHUNKS = 2
PAIRED_MOST = 8
VMEM = 56 * 1024 * 1024


def saturation_slope(x):
    small = jnp.exp(-jnp.abs(x))
    softplus = jnp.maximum(x, 0.0) + jnp.log1p(small)
    sigmoid = jnp.where(x >= 0, 1.0, small) / (1.0 + small)
    return sigmoid / (1.0 + softplus)


def delta_kernel(docs, x_ref, w_ref, winner_ref, grad_ref, delta_ref):
    rows, width = delta_ref.shape
    logits = lax.dot_general(
        x_ref[...], w_ref[...], (((1,), (1,)), ((), ())), preferred_element_type=jnp.float32
    )
    logits = logits.reshape(docs, rows // docs, width)
    codes = lax.broadcasted_iota(jnp.int32, logits.shape, 1)
    chosen = winner_ref[...][:, None, :] == codes
    picked = jnp.sum(jnp.where(chosen, logits, 0.0), axis=1)
    delta = grad_ref[...] * saturation_slope(picked)
    spread = jnp.where(chosen, delta[:, None, :], 0.0)
    delta_ref[...] = spread.reshape(rows, width).astype(jnp.bfloat16)


def term_deltas(rows, weight, winner, grad):
    count, width = rows.shape
    vocab = weight.shape[0]
    docs = winner.shape[0]
    return pl.pallas_call(
        functools.partial(delta_kernel, docs),
        grid=(pl.cdiv(vocab, V_TILE),),
        in_specs=[
            pl.BlockSpec((count, width), lambda i: (0, 0)),
            pl.BlockSpec((V_TILE, width), lambda i: (i, 0)),
            pl.BlockSpec((docs, V_TILE), lambda i: (0, i)),
            pl.BlockSpec((docs, V_TILE), lambda i: (0, i)),
        ],
        out_specs=pl.BlockSpec((count, V_TILE), lambda i: (0, i)),
        out_shape=jax.ShapeDtypeStruct((count, vocab), jnp.bfloat16),
        compiler_params=pltpu.CompilerParams(vmem_limit_bytes=VMEM),
        cost_estimate=pl.CostEstimate(
            flops=2 * count * vocab * width,
            bytes_accessed=2 * vocab * width + 2 * count * (vocab + width),
            transcendentals=0,
        ),
        name="term_deltas",
    )(rows, weight, winner, grad)


def weight_kernel(da_ref, db_ref, xa_ref, xb_ref, out_ref):
    dims = (((0,), (0,)), ((), ()))
    total = lax.dot_general(da_ref[...], xa_ref[...], dims, preferred_element_type=jnp.float32)
    total += lax.dot_general(db_ref[...], xb_ref[...], dims, preferred_element_type=jnp.float32)
    out_ref[...] = total.astype(jnp.bfloat16)


def weight_grads(delta_a, delta_b, rows_a, rows_b):
    count, vocab = delta_a.shape
    width = rows_a.shape[1]
    whole = pl.BlockSpec((count, width), lambda i: (0, 0))
    part = pl.BlockSpec((count, V_TILE), lambda i: (0, i))
    return pl.pallas_call(
        weight_kernel,
        grid=(pl.cdiv(vocab, V_TILE),),
        in_specs=[part, part, whole, whole],
        out_specs=pl.BlockSpec((V_TILE, width), lambda i: (i, 0)),
        out_shape=jax.ShapeDtypeStruct((vocab, width), jnp.bfloat16),
        compiler_params=pltpu.CompilerParams(vmem_limit_bytes=VMEM),
        cost_estimate=pl.CostEstimate(
            flops=4 * count * vocab * width,
            bytes_accessed=2 * vocab * width + 4 * count * (vocab + width),
            transcendentals=0,
        ),
        name="weight_grads",
    )(delta_a, delta_b, rows_a, rows_b)


TILE = 256
RELAY_CHUNKS = 2
BACK_WIDTH = 512
MESH = pl.DeviceIdType.MESH


def fused_kernel(
    hidden, route, winner, grad, weight,
    weight_grad, hidden_grad,
    near_pick, far_pick, far_route,
    relay, near_out, far_out, rows, delta, w_tiles, w_columns, g_tiles, landing, back_out, back_in,
    route_send, route_recv, relay_send, relay_recv, near_send, near_recv, far_send, far_recv,
    home_send, home_recv, part_send, part_recv, back_send, back_recv, tile_sem, column_sem, grad_sem,
):
    tokens, width = hidden.shape
    vocab = weight.shape[0]
    tiles, docs, _ = winner.shape
    near_docs = docs // 2
    count = near_out.shape[0]
    slot = count // near_docs
    peers = near_docs
    me = lax.axis_index("vocab")
    side = me // peers
    local = me % peers
    across = (me + peers) % (2 * peers)
    overlap = tiles * TILE - vocab

    def peer(k):
        flipped, scale = 0, 1
        while scale < peers:
            bit = local // scale % 2
            flipped = flipped + scale * ((1 - bit) if k & scale else bit)
            scale *= 2
        return side * peers + flipped

    def send(src, dst, send_sem, recv_sem, device):
        return pltpu.make_async_remote_copy(
            src_ref=src, dst_ref=dst, send_sem=send_sem, recv_sem=recv_sem,
            device_id={"vocab": device}, device_id_type=MESH,
        )

    def slots(k):
        return pl.ds(k * slot, slot)

    barrier = pltpu.get_barrier_semaphore()
    for k in range(1, peers):
        pl.semaphore_signal(barrier, inc=1, device_id={"vocab": peer(k)}, device_id_type=MESH)
    pl.semaphore_signal(barrier, inc=1, device_id={"vocab": across}, device_id_type=MESH)
    pl.semaphore_wait(barrier, peers)

    route_copy = send(route, far_route, route_send, route_recv, across)
    route_copy.start()
    relay_width = width // RELAY_CHUNKS
    relays = []
    for c in range(RELAY_CHUNKS):
        part = pl.ds(c * relay_width, relay_width)
        relays.append(
            send(hidden.at[:, part], relay.at[:, part], relay_send.at[c], relay_recv.at[c], across)
        )
        relays[c].start()

    def tile_copy(i, place):
        start = pl.multiple_of(i * TILE - i // (tiles - 1) * overlap, 16)
        return pltpu.make_async_copy(
            weight.at[pl.ds(start, TILE), :], w_tiles.at[place], tile_sem.at[place]
        )

    def column_copies(j, place):
        columns = pl.ds(pl.multiple_of(j * TILE, TILE), TILE)
        full = (tiles - 1) * TILE
        return (
            pltpu.make_async_copy(
                weight.at[pl.ds(0, full), columns],
                w_columns.at[place, pl.ds(0, full), :],
                column_sem.at[place, 0],
            ),
            pltpu.make_async_copy(
                weight.at[pl.ds(vocab - TILE, TILE), columns],
                w_columns.at[place, pl.ds(full, TILE), :],
                column_sem.at[place, 1],
            ),
        )

    def start_columns(j, place):
        for copy in column_copies(j, place):
            copy.start()

    def chooser(table):
        tile = lax.broadcasted_iota(jnp.int32, (peers, tokens), 0)
        tile = side * peers + (tile ^ local)
        listed = jnp.zeros((peers, tokens), jnp.bool_)
        for t in range(TOP):
            listed |= table[t : t + 1, :] == tile
        above = lax.broadcasted_iota(jnp.int32, (tokens, tokens), 0)
        below = lax.broadcasted_iota(jnp.int32, (tokens, tokens), 1)
        earlier = (above % BLOCK == 0) & (above // BLOCK < below // BLOCK)
        ranking = jnp.dot(
            jnp.where(listed, 1.0, 0.0).astype(jnp.bfloat16),
            jnp.where(earlier, 1.0, 0.0).astype(jnp.bfloat16),
            preferred_element_type=jnp.float32,
        ).astype(jnp.int32)
        place = jnp.where(listed, ranking, -1)
        shape = (peers, slot, tokens)
        entry = lax.broadcasted_iota(jnp.int32, shape, 1)
        token = lax.broadcasted_iota(jnp.int32, shape, 2)
        match = (place[:, None, :] == entry // BLOCK) & (entry % BLOCK == token % BLOCK)
        return jnp.where(match, 1.0, 0.0).reshape(count, tokens).astype(jnp.bfloat16)

    near_pick[...] = chooser(route[...])
    near_out[...] = jnp.dot(
        near_pick[...], hidden[...], preferred_element_type=jnp.float32
    ).astype(jnp.bfloat16)
    near_sends = []
    for k in range(1, peers):
        copy = send(
            near_out.at[slots(k), :], rows.at[slots(k), :], near_send.at[k], near_recv.at[k], peer(k)
        )
        copy.start()
        near_sends.append(copy)
    rows[pl.ds(0, slot), :] = near_out[pl.ds(0, slot), :]

    far_sends = []

    def pass_on(c):
        relays[c].wait_recv()
        part = pl.ds(c * relay_width, relay_width)
        far_out[:, part] = jnp.dot(
            far_pick[...], relay[:, part], preferred_element_type=jnp.float32
        ).astype(jnp.bfloat16)
        for k in range(1, peers):
            copy = send(
                far_out.at[slots(k), part],
                rows.at[pl.ds(count + k * slot, slot), part],
                far_send.at[c, k],
                far_recv.at[c, k],
                peer(k),
            )
            copy.start()
            far_sends.append(copy)
        rows[pl.ds(count, slot), part] = far_out[pl.ds(0, slot), part]

    def deltas(row, doc):
        tile_copy(0, 0).start()

        def body(i, carry):
            place = i % 2

            @pl.when(i + 1 < tiles)
            def _():
                tile_copy(i + 1, 1 - place).start()

            tile_copy(i, place).wait()
            logits = lax.dot_general(
                rows[pl.ds(row, count), :],
                w_tiles[place],
                (((1,), (1,)), ((), ())),
                preferred_element_type=jnp.float32,
            )
            logits = logits.reshape(near_docs, slot, TILE)
            codes = lax.broadcasted_iota(jnp.int32, logits.shape, 1)
            chosen = winner[i, pl.ds(doc, near_docs), :][:, None, :] == codes
            picked = jnp.sum(jnp.where(chosen, logits, 0.0), axis=1)
            term = grad[i, pl.ds(doc, near_docs), :] * saturation_slope(picked)
            spread = jnp.where(chosen, term[:, None, :], 0.0)
            delta[pl.ds(row, count), pl.ds(pl.multiple_of(i * TILE, TILE), TILE)] = spread.reshape(
                count, TILE
            ).astype(jnp.bfloat16)
            return carry

        lax.fori_loop(0, tiles, body, 0)

    columns = width // TILE

    def column_step(row, j, out, home):
        place = j % 2

        @pl.when(j + 1 < columns)
        def _():
            start_columns(j + 1, 1 - place)

        for copy in column_copies(j, place):
            copy.wait()
        value = jnp.dot(
            delta[pl.ds(row, count), :], w_columns[place], preferred_element_type=jnp.float32
        ).astype(jnp.bfloat16)
        where = pl.ds(pl.multiple_of(j * TILE, TILE), TILE)
        out[:, where] = value
        landing[home, pl.ds(0, slot), where] = value[:slot]

    route_copy.wait_recv()
    far_pick[...] = chooser(far_route[...])
    pass_on(0)
    for copy in near_sends:
        copy.wait_recv()
    start_columns(0, 0)
    deltas(0, 0)
    for c in range(1, RELAY_CHUNKS):
        pass_on(c)
    for copy in near_sends:
        copy.wait_send()

    def near_column(j, carry):
        column_step(0, j, near_out, 0)
        return carry

    lax.fori_loop(0, columns, near_column, 0)
    start_columns(0, 0)
    for copy in far_sends:
        copy.wait_recv()
    homes = []
    for k in range(1, peers):
        copy = send(
            near_out.at[slots(k), :],
            landing.at[0, slots(k), :],
            home_send.at[k],
            home_recv.at[k],
            peer(k),
        )
        copy.start()
        homes.append(copy)
    deltas(count, near_docs)
    for copy in far_sends:
        copy.wait_send()
    per_chunk = BACK_WIDTH // TILE
    chunks = width // BACK_WIDTH

    def part_copy(c, k):
        part = pl.ds(pl.multiple_of(c * BACK_WIDTH, BACK_WIDTH), BACK_WIDTH)
        return send(
            far_out.at[slots(k), part],
            landing.at[1, slots(k), part],
            part_send.at[c, k],
            part_recv.at[c, k],
            peer(k),
        )

    def far_columns(c, carry):
        for t in range(per_chunk):
            column_step(count, c * per_chunk + t, far_out, 1)
        for k in range(1, peers):
            part_copy(c, k).start()
        return carry

    lax.fori_loop(0, chunks, far_columns, 0)

    def back_copy(c):
        part = pl.ds(pl.multiple_of(c * BACK_WIDTH, BACK_WIDTH), BACK_WIDTH)
        return send(
            back_out.at[:, part], back_in.at[:, part], back_send.at[c], back_recv.at[c], across
        )

    gather = (((0,), (0,)), ((), ()))

    def pass_back(c):
        for k in range(1, peers):
            part_copy(c, k).wait()
        part = pl.ds(pl.multiple_of(c * BACK_WIDTH, BACK_WIDTH), BACK_WIDTH)
        back_out[:, part] = lax.dot_general(
            far_pick[...], landing[1, :, part], gather, preferred_element_type=jnp.float32
        ).astype(jnp.bfloat16)
        back_copy(c).start()

    def grad_copy(i, place):
        start = pl.multiple_of(i * TILE, TILE)
        return pltpu.make_async_copy(
            g_tiles.at[place], weight_grad.at[pl.ds(start, TILE), :], grad_sem.at[place]
        )

    def grad_tile(i):
        return lax.dot_general(
            delta[:, pl.ds(pl.multiple_of(i * TILE, TILE), TILE)],
            rows[...],
            gather,
            preferred_element_type=jnp.float32,
        ).astype(jnp.bfloat16)

    def grad_body(i, carry):
        place = i % 2

        @pl.when(i >= 2)
        def _():
            grad_copy(i - 2, place).wait()

        g_tiles[place] = grad_tile(i)
        grad_copy(i, place).start()

        @pl.when((i % 2 == 1) & (i // 2 < chunks))
        def _():
            pass_back(i // 2)

        return carry

    lax.fori_loop(0, tiles - 1, grad_body, 0)
    last = tiles - 1
    grad_copy(last - 2, last % 2).wait()
    g_tiles[last % 2] = grad_tile(last)
    tail = pltpu.make_async_copy(
        g_tiles.at[last % 2, pl.ds(overlap, TILE - overlap), :],
        weight_grad.at[pl.ds(last * TILE, TILE - overlap), :],
        grad_sem.at[last % 2],
    )
    tail.start()
    for copy in homes:
        copy.wait()

    def finish(c, carry):
        back_copy(c).wait()
        part = pl.ds(pl.multiple_of(c * BACK_WIDTH, BACK_WIDTH), BACK_WIDTH)
        own = lax.dot_general(
            near_pick[...], landing[0, :, part], gather, preferred_element_type=jnp.float32
        )
        hidden_grad[:, part] = (own + back_in[:, part].astype(jnp.float32)).astype(jnp.bfloat16)
        return carry

    lax.fori_loop(0, chunks, finish, 0)
    route_copy.wait_send()
    for copy in relays:
        copy.wait_send()
    grad_copy(last - 1, (last - 1) % 2).wait()
    tail.wait()


def fused(hidden, route, winner, grad, weight, slot_rows):
    tokens, width = hidden.shape
    vocab = weight.shape[0]
    tiles, docs, _ = winner.shape
    peers = docs // 2
    count = peers * slot_rows
    chunks = width // BACK_WIDTH
    held = jnp.bfloat16
    dma = pltpu.SemaphoreType.DMA
    vmem = pl.BlockSpec(memory_space=pltpu.VMEM)
    hbm = pl.BlockSpec(memory_space=pl.ANY)
    return pl.pallas_call(
        fused_kernel,
        in_specs=[vmem] * 4 + [hbm],
        out_specs=[hbm, vmem],
        out_shape=[
            jax.ShapeDtypeStruct((vocab, width), held),
            jax.ShapeDtypeStruct((tokens, width), held),
        ],
        scratch_shapes=[
            pltpu.VMEM((count, tokens), held),
            pltpu.VMEM((count, tokens), held),
            pltpu.VMEM(route.shape, jnp.int32),
            pltpu.VMEM((tokens, width), held),
            pltpu.VMEM((count, width), held),
            pltpu.VMEM((count, width), held),
            pltpu.VMEM((2 * count, width), held),
            pltpu.VMEM((2 * count, tiles * TILE), held),
            pltpu.VMEM((2, TILE, width), held),
            pltpu.VMEM((2, tiles * TILE, TILE), held),
            pltpu.VMEM((2, TILE, width), held),
            pltpu.VMEM((2, count, width), held),
            pltpu.VMEM((tokens, width), held),
            pltpu.VMEM((tokens, width), held),
            dma, dma,
            dma((RELAY_CHUNKS,)), dma((RELAY_CHUNKS,)),
            dma((peers,)), dma((peers,)),
            dma((RELAY_CHUNKS, peers)), dma((RELAY_CHUNKS, peers)),
            dma((peers,)), dma((peers,)),
            dma((chunks, peers)), dma((chunks, peers)),
            dma((chunks,)), dma((chunks,)),
            dma((2,)), dma((2, 2)), dma((2,)),
        ],
        compiler_params=pltpu.CompilerParams(
            collective_id=0, has_side_effects=True, vmem_limit_bytes=62 * 1024 * 1024
        ),
        name="fused",
    )(hidden, route, winner, grad, weight)


def tiled(x, blank):
    vocab = x.shape[1]
    tiles = pl.cdiv(vocab, TILE)
    full = (tiles - 1) * TILE
    tail = x[:, vocab - TILE :]
    if blank:
        fresh = jnp.arange(TILE) >= tiles * TILE - vocab
        tail = jnp.where(fresh[None, :], tail, 0)
    whole = jnp.concatenate([x[:, :full], tail], axis=1)
    return whole.reshape(x.shape[0], tiles, TILE).swapaxes(0, 1)


def on_device(hidden, head_weight, term_grad, winner, route):
    n = lax.axis_size("vocab")
    half = n // 2
    me = lax.axis_index("vocab")
    tokens, width = hidden.shape
    block_count = route.shape[0]
    capacity = 2 * max(1, block_count * route.shape[1] // n)
    slot_rows = capacity * BLOCK
    base = me // half * half
    peers = jnp.arange(half, dtype=jnp.int32)
    paired = half <= PAIRED_MOST and half & (half - 1) == 0
    if paired:
        peers = peers ^ (me % half)
    near, far = base + peers, (half - base) + peers

    def cross(x):
        return lax.ppermute(x, "vocab", [(i, (i + half) % n) for i in range(n)])

    def exchange(pieces):
        if not paired:
            sides = [list(range(half)), list(range(half, n))]
            return list(lax.all_to_all(pieces, "vocab", 0, 0, axis_index_groups=sides, tiled=True))
        pieces = list(pieces)
        return [pieces[0]] + [
            lax.ppermute(pieces[k], "vocab", [(i, i ^ k) for i in range(n)])
            for k in range(1, half)
        ]

    def chooser(table):
        listed = jnp.any(table[:, :, None] == near[None, None, :], axis=1)
        ranking = jnp.cumsum(listed.astype(jnp.int32), axis=0) - 1
        slot = jnp.where(listed, ranking, -1)
        slots = jnp.arange(half * slot_rows, dtype=jnp.int32)
        place = jnp.arange(tokens, dtype=jnp.int32)
        wanted = jnp.repeat(jnp.repeat(slot.T, BLOCK, axis=1), slot_rows, axis=0)
        match = wanted == (slots % slot_rows // BLOCK)[:, None]
        match &= (slots % BLOCK)[:, None] == (place % BLOCK)[None, :]
        return match.astype(jnp.bfloat16)

    def select(pick, rows):
        chosen = jnp.dot(pick, rows, preferred_element_type=jnp.float32).astype(jnp.bfloat16)
        return chosen.reshape(half, slot_rows, rows.shape[1])

    def gather_back(pick, parts):
        return lax.dot_general(
            pick,
            jnp.concatenate(parts, axis=0),
            (((0,), (0,)), ((), ())),
            preferred_element_type=jnp.float32,
        )

    out_step = width // OUT_CHUNKS
    back_step = width // BACK_CHUNKS
    if paired and slot_rows % 16 == 0:
        order = jnp.concatenate([near, far])
        listing = jnp.repeat(route.T, BLOCK, axis=1)
        listing = jnp.pad(listing, ((0, -route.shape[1] % 8), (0, 0)), constant_values=-1)
        return tuple(
            fused(
                hidden,
                listing,
                tiled(winner[order], False),
                tiled(term_grad[order], True),
                head_weight,
                slot_rows,
            )
        )
    far_route = cross(route)
    near_pick, far_pick = chooser(route), chooser(far_route)
    far_hidden = [cross(hidden[:, c * out_step : (c + 1) * out_step]) for c in range(OUT_CHUNKS)]
    near_rows = jnp.concatenate(exchange(select(near_pick, hidden)), axis=0)
    far_rows = [
        jnp.concatenate(exchange(select(far_pick, piece)), axis=0) for piece in far_hidden
    ]
    far_rows = jnp.concatenate(far_rows, axis=1)

    near_delta = term_deltas(near_rows, head_weight, winner[near], term_grad[near])
    far_delta = term_deltas(far_rows, head_weight, winner[far], term_grad[far])

    def parts(delta, c):
        value = jnp.dot(
            delta,
            head_weight[:, c * back_step : (c + 1) * back_step],
            preferred_element_type=jnp.float32,
        ).astype(jnp.bfloat16)
        return exchange(value.reshape(half, slot_rows, back_step))

    far_sum = [
        cross(gather_back(far_pick, parts(far_delta, c)).astype(jnp.bfloat16))
        for c in range(BACK_CHUNKS)
    ]
    near_sum = [gather_back(near_pick, parts(near_delta, c)) for c in range(BACK_CHUNKS)]
    hidden_grad = jnp.concatenate(
        [
            (a + b.astype(jnp.float32)).astype(jnp.bfloat16)
            for a, b in zip(near_sum, far_sum)
        ],
        axis=1,
    )
    weight_grad = weight_grads(near_delta, far_delta, near_rows, far_rows)
    return (weight_grad, hidden_grad)


def solution(mesh):
    placed = (
        P(("groups", "vocab"), None),
        P("vocab", None),
        P("groups", "vocab"),
        P("groups", "vocab"),
        P(("groups", "vocab"), None),
    )
    return jax.shard_map(
        on_device,
        mesh=mesh,
        in_specs=placed,
        out_specs=(P(("groups", "vocab"), None), P(("groups", "vocab"), None)),
        check_vma=False,
    )
```
